1024 devices in a mesh: dp: 4 (over x), expert: 16 (over z), tensor: 16 (over y, core).
Axes of the slice: x: 4, y: 8, z: 16, core: 2. Of those that a mesh axis runs over, the one named last changes fastest.
Arguments:
- grad_out: bfloat16 [8192, 7168], P(('dp', 'expert'), 'tensor'), may hold values from -6 to 6
- route_ids: int32 [8192, 2], P(('dp', 'expert')), may hold values from 0 to 15, all different within a row; in each aligned block of 128 rows (0 to 127, 128 to 255, ...) at most 24 rows name the same one
- route_gates: float32 [8192, 2], P(('dp', 'expert')), may hold values from 0.05 to 1
- hidden_acts: bfloat16 [4, 16, 384, 4864], P('dp', 'expert'), may hold values from -0.29882812 to 0.29882812
- down_weight: bfloat16 [16, 4864, 7168], P('expert', None, 'tensor'), may hold values from -0.078125 to 0.078125
Outputs:
- grad_weight: bfloat16 [16, 4864, 7168], P('expert', 'dp', 'tensor')
- grad_hidden: bfloat16 [4, 16, 384, 4864], P('dp', 'expert', None, 'tensor')
The draws below stay inside these ranges and needn't reach their ends.
Inputs may be any that keep to these rules, and one draw needn't show every extreme that they name: `route_ids`: in each aligned block of 128 rows (the tokens of one group) no expert is named by more than 24 rows, a bound that some block reaches; the two experts of a row differ.
All inputs are finite; a program needn't handle non-finite values.
Results may differ from the reference program's by a relative error of at most 0.022.
Values may be sent and summed in bfloat16 or wider, within the bound.
A program may use at most 64 MiB of HBM per device.

```python
import math
import jax
import jax.numpy as jnp
import numpy as np
from jax import lax

D = 7168
FF = 4864
TG = 128
EXPERTS = 16
CAP = 24
SLOTS = 384
TOKENS = 8192
N_DP = 4
N_EXPERT = 16
N_TENSOR = 16


def steps_of(key, extent, shards, least, largest):
    def one(position, parts):
        heights = jax.random.uniform(jax.random.fold_in(jax.random.fold_in(key, 6), position), (parts,), jnp.float32, least / len(shards), largest / len(shards))
        return jnp.repeat(jnp.exp(heights), extent[position] // parts).reshape((-1,) + (1,) * (len(extent) - position - 1))

    factor_of = one(*shards[0])
    for cut in shards[1:]:
        factor_of = factor_of * one(*cut)
    return factor_of


def assign_block(own_key, own, number, rows, amount, top, reach, slope):
    sequence = jax.random.permutation(own_key, amount)
    heavy_load, usual = portions_of(amount, rows * top, reach, slope, True), portions_of(amount, rows * top, reach, slope, False)
    places = jnp.arange(amount)

    def named(tallies, offset_by):
        used = int((tallies > 0).sum())
        fixed = max(1, used // 4)
        passed = fixed + (places - fixed + offset_by * (used - fixed)) % max(1, amount - fixed)
        return jnp.zeros((amount,), jnp.int32).at[sequence[jnp.where(places < fixed, places, passed)]].set(jnp.asarray(tallies, jnp.int32))

    tallies = jnp.where(number % 4 == 0, named(heavy_load, number // 4), named(usual, number - number // 4 - 1))
    mixed = jax.random.permutation(jax.random.fold_in(own, 3), amount)
    donor, sink = mixed[0:amount // 2 * 2:2], mixed[1:amount // 2 * 2:2]
    room = jnp.minimum(tallies[donor] - 1, reach - tallies[sink]) // 2
    room = jnp.where((donor == sequence[0]) | (sink == sequence[0]) | (tallies[sink] == 0), 0, jnp.maximum(room, 0))
    passed = jax.random.randint(jax.random.fold_in(own, 4), (amount // 2,), 0, 1 << 20) % (room + 1)
    tallies = tallies.at[donor].add(-passed).at[sink].add(passed)
    items = jnp.searchsorted(jnp.cumsum(tallies), jnp.arange(rows * top), side="right").astype(jnp.int32)
    grid = items.reshape(top, rows).T
    grid = grid[jax.random.permutation(jax.random.fold_in(own, 1), rows)]
    offset_by = jax.random.randint(jax.random.fold_in(own, 2), (rows, 1), 0, top)
    return jnp.take_along_axis(grid, (jnp.arange(top)[None, :] + offset_by) % top, axis=1)


def portions_of(number_of, total, most, skew, full):
    weights = [(1 << 20) // math.isqrt(rank ** skew) + 1 for rank in range(1, number_of + 1)]
    largest = most if full else min(most, max(-(-total // number_of), total * weights[0] // sum(weights)))
    least = 1 if total - largest >= number_of - 1 else 0
    given, spare = [largest] + [least] * (number_of - 1), total - largest - least * (number_of - 1)
    while spare > 0:
        candidates = [i for i in range(1, number_of) if given[i] < largest] or [i for i in range(1, number_of) if given[i] < most]
        mass, budget = sum([weights[i] for i in candidates]), spare
        for i in candidates:
            addition = min(most - given[i], max(1, budget * weights[i] // mass), spare)
            given[i] = given[i] + addition
            spare = spare - addition
    return np.array(given)


def normal_values(key, shape, deviation, reach, pieces=(), kind=jnp.bfloat16):
    result = deviation * jax.random.normal(key, shape, jnp.float32)
    if pieces:
        result = result * steps_of(key, shape, pieces, -0.22, 0.18)
    return jnp.clip(result, -reach, reach).astype(kind)


def setup_inputs(seed: int = 0) -> dict:
    key_list = jax.random.split(jax.random.key(seed), 6)
    grad_out = normal_values(key_list[0], (TOKENS, D), 1.0, 6.0, ((0, 64), (1, 16)))
    route_ids_keys = jax.random.split(jax.random.fold_in(key_list[1], 1), TOKENS // TG)
    route_ids_turns = jax.random.permutation(jax.random.fold_in(key_list[1], 3), TOKENS // TG)
    route_ids = jax.vmap(lambda own, number: assign_block(jax.random.fold_in(key_list[1], 2), own, number, TG, EXPERTS, 2, CAP, 2))(route_ids_keys, route_ids_turns).reshape((TOKENS, 2))
    route_gates = jnp.clip(0.05 + 0.95 * jax.random.uniform(key_list[2], (TOKENS, 2), jnp.float32) ** steps_of(key_list[2], (TOKENS, 2), ((0, 64),), -0.2, 0.2), 0.05, 1.0)
    hidden_acts = normal_values(key_list[3], (N_DP, EXPERTS, SLOTS, FF), 0.05, 0.29882812, ((0, 4), (1, 16)))
    down_weight = normal_values(key_list[4], (EXPERTS, FF, D), FF ** -0.5, 0.078125, ((0, 16), (2, 16)))
    return {"grad_out": grad_out, "route_ids": route_ids, "route_gates": route_gates, "hidden_acts": hidden_acts, "down_weight": down_weight}


def route_rows(grad_out, route_ids, route_gates):
    groups = N_DP * N_EXPERT
    ids_grouped = route_ids.reshape(groups, TG * 2)
    onehot = (ids_grouped[:, :, None] == jnp.arange(EXPERTS, dtype=jnp.int32)[None, None, :]).astype(jnp.int32)
    before = jnp.cumsum(onehot, axis=1) - onehot
    slot_index = lax.optimization_barrier(jnp.sum(before * onehot, axis=2))
    source = (jnp.arange(groups, dtype=jnp.int32) % N_EXPERT)[:, None]
    targets = (ids_grouped * SLOTS + source * CAP + slot_index).astype(jnp.int32)
    targets = targets.reshape(N_DP, N_EXPERT * TG * 2)
    gate_vals = route_gates.reshape(N_DP, N_EXPERT * TG, 2)
    token_rows = grad_out.reshape(N_DP, N_EXPERT * TG, D)

    def dispatch(packed):
        target_row, gate_row, grad_rows = packed
        values = (gate_row[:, :, None] * grad_rows[:, None, :].astype(jnp.float32)).astype(jnp.bfloat16)
        values = values.reshape(N_EXPERT * TG * 2, D)
        return jnp.zeros((EXPERTS * SLOTS, D), jnp.bfloat16).at[target_row].set(values)
    routed = lax.map(dispatch, (targets, gate_vals, token_rows))
    return routed.reshape(N_DP, EXPERTS, SLOTS, D)

def reference(grad_out, route_ids, route_gates, hidden_acts, down_weight):
    routed = route_rows(grad_out, route_ids, route_gates)
    routed_by_expert = jnp.transpose(routed, (1, 0, 2, 3))
    acts_by_expert = jnp.transpose(hidden_acts, (1, 0, 2, 3))

    def weight_grad(packed):
        activations, grad_rows = packed
        summed = jnp.zeros((FF, D), jnp.float32)
        for group in range(N_DP):
            product = jnp.dot(activations[group].T, grad_rows[group], preferred_element_type=jnp.float32)
            product = lax.optimization_barrier(product.astype(jnp.bfloat16))
            summed = summed + product.astype(jnp.float32)
        return summed.astype(jnp.bfloat16)
    grad_weight = lax.map(weight_grad, (acts_by_expert, routed_by_expert))

    def hidden_grad(packed):
        weight, grad_rows = packed
        weight_split = weight.astype(jnp.float32).reshape(FF, N_TENSOR, D // N_TENSOR)
        results = []
        for group in range(N_DP):
            rows_split = grad_rows[group].astype(jnp.float32).reshape(SLOTS, N_TENSOR, D // N_TENSOR)
            blocks = jnp.einsum('snc,fnc->nsf', rows_split, weight_split, precision=lax.Precision.HIGHEST)
            blocks = lax.optimization_barrier(blocks.astype(jnp.bfloat16))
            results.append(lax.optimization_barrier(jnp.sum(blocks.astype(jnp.float32), axis=0)).astype(jnp.bfloat16))
        return jnp.stack(results)
    hidden_all = lax.map(hidden_grad, (down_weight, routed_by_expert))
    grad_hidden = jnp.transpose(hidden_all, (1, 0, 2, 3))
    return (grad_weight, grad_hidden)
```

```python
import jax
import jax.numpy as jnp
from jax import lax
from jax.experimental import pallas as pl
from jax.experimental.pallas import tpu as pltpu
from jax.sharding import PartitionSpec as P

BF, F32 = jnp.bfloat16, jnp.float32
MESH = pl.DeviceIdType.MESH
HOPS = (0, 1, -1, 2, -2, 3, -3, 4, -4, 5, -5, 6, -6, 7, -7, 8)
TURNS = (4, 3, -3, 2, -2, 1, -1, 0)
GROUPS = ((0, 256), (256, 128))
CAP = 24


def dot(a, b, dims=((1,), (0,))):
    return lax.dot_general(a, b, (dims, ((), ())), preferred_element_type=F32)


def kernel(
    ids, gates, grad_t, acts, weight_t, gw_out, gh_out,
    staged, weight, acts_buf, fwd, outgoing, arrived, rows32, named, perm, total,
    rt0, rt1, peers0, peers1, own0, own1, give0, give1, take0, take1,
    pa0, pa1, pb0, pb1, ma0, ma1, mb0, mb1,
    send_sems, recv_sems, local_sems,
):
    nx, nz, nt = lax.axis_size("dp"), lax.axis_size("expert"), lax.axis_size("tensor")
    ny = nt // 2
    x, z, t = lax.axis_index("dp"), lax.axis_index("expert"), lax.axis_index("tensor")
    core = lax.rem(t, 2)
    y = lax.div(t, 2)
    right, left = {"dp": lax.rem(x + 1, nx)}, {"dp": lax.rem(x + nx - 1, nx)}
    up, down = {"tensor": lax.rem(t + 2, nt)}, {"tensor": lax.rem(t + nt - 2, nt)}
    twin = {"tensor": t + 1 - 2 * core}
    chunk = weight.shape[0] // nt
    part_a = (chunk // 2 + 15) // 16 * 16
    rows_a, rows_b = pl.ds(0, part_a), pl.ds(part_a, chunk - part_a)
    rt, peers, own, give, take = (rt0, rt1), (peers0, peers1), (own0, own1), (give0, give1), (take0, take1)
    pa, pb, ma, mb = (pa0, pa1), (pb0, pb1), (ma0, ma1), (mb0, mb1)
    count = [0]
    started = []

    def remote(src, dst, device):
        n = count[0]
        count[0] += 1
        return pltpu.make_async_remote_copy(
            src_ref=src, dst_ref=dst, send_sem=send_sems.at[n], recv_sem=recv_sems.at[n],
            device_id=device, device_id_type=MESH,
        )

    def start(copy):
        copy.start()
        started.append(copy)

    width = acts_buf.shape[3]
    load_weight = pltpu.make_async_copy(weight_t, staged, local_sems.at[0])
    load_weight.start()

    def column(owner, half):
        return pl.multiple_of((19 * owner // 2) * 128 + half * width, 128)

    loads = []
    for half in range(2):
        load = pltpu.make_async_copy(acts.at[:, pl.ds(column(x, half), width)], acts_buf.at[0, half], local_sems.at[1 + half])
        load.start()
        loads.append(load)

    barrier = pltpu.get_barrier_semaphore()
    experts = [lax.rem(z + nz - h, nz) for h in HOPS]
    greeted = [right, left, up, down, twin] + [{"expert": e} for e in experts[1:]]
    for device in greeted:
        pl.semaphore_signal(barrier, inc=1, device_id=device, device_id_type=MESH)

    id0, id1 = ids[0:1, :], ids[1:2, :]
    gate0, gate1 = gates[0:1, :], gates[1:2, :]
    tokens = ids.shape[1]
    for j, e in enumerate(experts):
        named[j : j + 1, :] = ((id0 == e) | (id1 == e)).astype(F32)
    earlier = lax.broadcasted_iota(jnp.int32, (tokens, tokens), 0) < lax.broadcasted_iota(jnp.int32, (tokens, tokens), 1)
    slots = dot(named[...].astype(BF), earlier.astype(F32).astype(BF)).astype(jnp.int32)
    place = lax.broadcasted_iota(jnp.int32, (CAP, tokens), 0)
    picks, scales = [], []
    for j, e in enumerate(experts):
        here = (slots[j : j + 1, :] == place) & (named[j : j + 1, :] > 0.5)
        gate = jnp.where(id0 == e, gate0, 0.0) + jnp.where(id1 == e, gate1, 0.0)
        picks.append(jnp.where(here, 1.0, 0.0))
        scales.append(jnp.sum(jnp.where(here, gate, 0.0), axis=1, keepdims=True))
    pick = jnp.concatenate(picks, axis=0).astype(BF)
    features = grad_t.shape[0]
    padded = rows32.shape[1]
    padded_grad = jnp.concatenate([grad_t[...], jnp.zeros((padded - features, tokens), BF)], axis=0)
    rows32[...] = dot(pick, padded_grad, ((1,), (1,))) * jnp.concatenate(scales, axis=0)
    lanes = padded // 128
    for j in range(nz):
        block = jnp.concatenate([rows32[CAP * j : CAP * (j + 1), 128 * i : 128 * (i + 1)] for i in range(lanes)], axis=0)
        if j == 0:
            arrived[0] = block.astype(BF)
        else:
            outgoing[j] = block.astype(BF)

    pl.semaphore_wait(barrier, len(greeted))

    to_expert = [None] + [remote(outgoing.at[j], arrived.at[j], {"expert": experts[j]}) for j in range(1, nz)]
    for copy in to_expert[1:]:
        start(copy)

    rows_here = acts.shape[0] // 2
    quarter = rows_here // 2
    first = pl.multiple_of(lax.rem(y, 2) * rows_here, 16)
    other = pl.multiple_of((1 - lax.rem(y, 2)) * rows_here, 16)
    far = lax.rem(x + 2, nx)
    x_near = []
    for q, device, owner in ((1, right, lax.rem(x + 1, nx)), (2, left, lax.rem(x + nx - 1, nx))):
        x_near.append(remote(
            acts.at[pl.ds(first, rows_here), pl.ds(column(owner, core), width)],
            acts_buf.at[q, core, pl.ds(first, rows_here), :], device,
        ))
    x_half, x_far = [], []
    for k, device in ((0, right), (1, left)):
        here = pl.ds(pl.multiple_of(first + k * quarter, 16), quarter)
        x_half.append(remote(acts.at[here, pl.ds(column(far, core), width)], fwd.at[k], device))
        x_far.append(remote(fwd.at[k], acts_buf.at[3, core, here, :], device))
    for copy in x_near + x_half:
        start(copy)
    y_part, twin_part = {}, {}
    for q in (1, 2, 3):
        for k, device in ((0, up), (1, down)):
            here = acts_buf.at[q, core, pl.ds(pl.multiple_of(first + k * quarter, 16), quarter), :]
            there = acts_buf.at[q, core, pl.ds(pl.multiple_of(other + k * quarter, 16), quarter), :]
            y_part[q, k] = remote(here, here, device)
            twin_part[q, k] = remote(there, there, twin)
        here = acts_buf.at[q, core, pl.ds(first, rows_here), :]
        twin_part[q, 2] = remote(here, here, twin)

    load_weight.wait()

    def turn(i, carry):
        at = pl.multiple_of(i * 128, 128)
        weight[pl.ds(at, 128), :] = staged[:, pl.ds(at, 128)].astype(F32).T.astype(BF)
        return carry

    lax.fori_loop(0, weight.shape[0] // 128, turn, 0)

    slot_count = perm.shape[1]
    stands = lax.broadcasted_iota(jnp.int32, (CAP, slot_count), 1) - lax.broadcasted_iota(jnp.int32, (CAP, slot_count), 0)
    perm[...] = jnp.concatenate(
        [jnp.where(stands == CAP * lax.rem(z + nz + h, nz), 1.0, 0.0) for h in HOPS], axis=0
    ).astype(BF)

    def near_acts():
        for q in (1, 2):
            x_near[q - 1].wait_recv()
            start(y_part[q, 0])
            start(y_part[q, 1])
            start(twin_part[q, 2])

    def half_acts():
        for k in range(2):
            x_half[k].wait_recv()
            start(x_far[k])

    def far_acts():
        for k in range(2):
            x_far[k].wait_recv()
            start(y_part[3, k])
        start(twin_part[3, 2])

    def shared_acts(q):
        for k in range(2):
            y_part[q, k].wait_recv()
            start(twin_part[q, k])

    to_peers = []
    for g, (low, size) in enumerate(GROUPS):
        top, bottom = pl.ds(0, features // 2), pl.ds(features // 2, features // 2)
        to_peers.append((
            remote(rt[g], peers[g].at[0], right),
            remote(rt[g], peers[g].at[1], left),
            remote(peers[g].at[0, top, :], peers[g].at[2, top, :], right),
            remote(peers[g].at[1, bottom, :], peers[g].at[2, bottom, :], left),
        ))
    unpacked = [0]

    def collect(g):
        low, size = GROUPS[g]
        until = -(-(low + size) // CAP)
        for j in range(unpacked[0], until):
            if j:
                to_expert[j].wait_recv()
            block = arrived[j].astype(F32)
            for i in range(lanes):
                rows32[CAP * j : CAP * (j + 1), 128 * i : 128 * (i + 1)] = block[CAP * i : CAP * (i + 1), :]
        unpacked[0] = until
        rt[g][...] = rows32[low : low + size, :].T[:features, :].astype(BF)
        start(to_peers[g][0])
        start(to_peers[g][1])

    def pass_on(g):
        for k in range(2):
            to_peers[g][k].wait_recv()
            start(to_peers[g][2 + k])

    index = {turn_: i for i, turn_ in enumerate(TURNS)}
    index[-4] = index[4]
    to_twin, rings = [], []
    for g in range(len(GROUPS)):
        to_twin.append([remote(give[g].at[i], take[g].at[i], twin) for i in range(ny)])
        ring = {}
        for s in range(4):
            ring["pa", s] = remote(own[g].at[index[4 - s], rows_a, :], pa[g].at[s], up)
            ring["mb", s] = remote(own[g].at[index[s - 4], rows_b, :], mb[g].at[s], down)
        for s in range(3):
            ring["pb", s] = remote(own[g].at[index[3 - s], rows_b, :], pb[g].at[s], up)
            ring["ma", s] = remote(own[g].at[index[s - 3], rows_a, :], ma[g].at[s], down)
        rings.append(ring)

    def product(g, i, side):
        at = pl.multiple_of(chunk * (2 * lax.rem(y + ny + TURNS[i], ny) + side), 16)
        return dot(weight[pl.ds(at, chunk), :], rt[g][...]).astype(BF)

    def prepare(g, *which):
        for i in which:
            give[g][i] = product(g, i, 1 - core)
            start(to_twin[g][i])
            own[g][i] = product(g, i, core)

    def join(g, *which):
        for i in which:
            to_twin[g][i].wait_recv()
            own[g][i] = (own[g][i].astype(F32) + take[g][i].astype(F32)).astype(BF)

    def step(g, name, s):
        ring = rings[g]
        ring[name, s].wait_recv()
        buffer = {"pa": pa, "pb": pb, "ma": ma, "mb": mb}[name][g]
        rows = rows_a if name[1] == "a" else rows_b
        reach = {"pa": 3 - s, "pb": 2 - s, "ma": s - 2, "mb": s - 3}[name]
        i = index[reach]
        own[g][i, rows, :] = (own[g][i, rows, :].astype(F32) + buffer[s].astype(F32)).astype(BF)
        start(ring[name, s + 1])

    def stage0(g):
        prepare(g, 0, 1, 2)
        join(g, 0)
        start(rings[g]["pa", 0])
        start(rings[g]["mb", 0])
        join(g, 1, 2)
        start(rings[g]["pb", 0])
        start(rings[g]["ma", 0])

    def stage1(g):
        prepare(g, 3, 4)
        join(g, 3, 4)
        for name in ("pa", "mb", "pb", "ma"):
            step(g, name, 0)

    def stage2(g):
        prepare(g, 5, 6)
        join(g, 5, 6)
        for name in ("pa", "mb", "pb", "ma"):
            step(g, name, 1)

    def stage3(g):
        prepare(g, 7)
        join(g, 7)
        step(g, "pa", 2)
        step(g, "mb", 2)

    def finish(g):
        low, size = GROUPS[g]
        ring = rings[g]
        for name, s in (("pb", 2), ("ma", 2), ("pa", 3), ("mb", 3)):
            ring[name, s].wait_recv()
        i = index[0]
        share_a = own[g][i, rows_a, :].astype(F32) + (pa[g][3].astype(F32) + ma[g][2].astype(F32))
        share_b = own[g][i, rows_b, :].astype(F32) + (pb[g][2].astype(F32) + mb[g][3].astype(F32))
        return jnp.concatenate([share_a, share_b], axis=0).astype(BF)

    def weight_grad(q):
        both = [r[...] for r in rt] if q == 0 else [r[q - 1] for r in peers]
        ordered = sum(dot(b, perm[low : low + size, :]) for b, (low, size) in zip(both, GROUPS)).astype(BF)
        for half in range(2):
            columns = pl.ds(half * width, width)
            added = dot(ordered, acts_buf[q, half])
            if q == 0:
                total[:, columns] = added
            elif q < 3:
                total[:, columns] += added
            else:
                gw_out[:, columns] = (total[:, columns] + added).astype(BF)

    near_acts()
    half_acts()
    collect(0)
    stage0(0)
    far_acts()
    stage1(0)
    shared_acts(1)
    shared_acts(2)
    stage2(0)
    pass_on(0)
    collect(1)
    prepare(1, 0, 1, 2)
    stage3(0)
    join(1, 0)
    start(rings[1]["pa", 0])
    start(rings[1]["mb", 0])
    join(1, 1, 2)
    start(rings[1]["pb", 0])
    start(rings[1]["ma", 0])
    shared_acts(3)
    pass_on(1)
    stage1(1)
    done0 = finish(0)
    gh = dot(done0, perm[0 : GROUPS[0][1], :])
    stage2(1)
    for load in loads:
        load.wait()
    weight_grad(0)
    stage3(1)
    for q in (1, 2):
        for k in range(3):
            twin_part[q, k].wait_recv()
        weight_grad(q)
    done1 = finish(1)
    gh_out[...] = (gh + dot(done1, perm[GROUPS[1][0] :, :])).astype(BF)
    for k in range(3):
        twin_part[3, k].wait_recv()
    for g in range(len(GROUPS)):
        for k in range(2):
            to_peers[g][2 + k].wait_recv()
    weight_grad(3)
    for copy in started:
        copy.wait_send()


def routed_backward(ids, gates, grad_t, acts, weight_t):
    features, hidden = weight_t.shape
    slots = acts.shape[0]
    nx, nz, nt = lax.axis_size("dp"), lax.axis_size("expert"), lax.axis_size("tensor")
    width, chunk = 640, hidden // nt
    part_a = (chunk // 2 + 15) // 16 * 16
    part_b = chunk - part_a
    padded = -(-features // 128) * 128
    block = CAP * padded // 128
    sizes = [size for _, size in GROUPS]
    vmem = pltpu.VMEM
    scratch = [
        vmem((features, hidden), BF),
        vmem((hidden, features), BF),
        vmem((nx, 2, slots, width), BF),
        vmem((2, slots // 4, width), BF),
        vmem((nz, block, 128), BF),
        vmem((nz, block, 128), BF),
        vmem((slots, padded), F32),
        vmem((nz, ids.shape[1]), F32),
        vmem((slots, slots), BF),
        vmem((features, 2 * width), F32),
    ]
    scratch += [vmem((features, n), BF) for n in sizes]
    scratch += [vmem((3, features, n), BF) for n in sizes]
    for _ in range(3):
        scratch += [vmem((nt // 2, chunk, n), BF) for n in sizes]
    for hops, rows in ((4, part_a), (3, part_b), (3, part_a), (4, part_b)):
        scratch += [vmem((hops, rows, n), BF) for n in sizes]
    copies = (nz - 1) + 6 + 15 + 8 + 2 * (nt // 2 + 14)
    scratch += [
        pltpu.SemaphoreType.DMA((copies,)),
        pltpu.SemaphoreType.DMA((copies,)),
        pltpu.SemaphoreType.DMA((3,)),
    ]
    whole = pl.BlockSpec(memory_space=pltpu.VMEM)
    away = pl.BlockSpec(memory_space=pl.ANY)
    return pl.pallas_call(
        kernel,
        out_shape=(
            jax.ShapeDtypeStruct((features, 2 * width), BF),
            jax.ShapeDtypeStruct((chunk, slots), BF),
        ),
        in_specs=[whole, whole, whole, away, away],
        out_specs=(whole, whole),
        scratch_shapes=scratch,
        compiler_params=pltpu.CompilerParams(
            collective_id=0, has_side_effects=True, vmem_limit_bytes=52 * 1024 * 1024
        ),
        cost_estimate=pl.CostEstimate(flops=7 * 10**9, bytes_accessed=2 * 10**7, transcendentals=0),
    )(ids, gates, grad_t, acts, weight_t)


def on_device(grad_out, route_ids, route_gates, hidden_acts, down_weight):
    weight_grad, hidden_grad = routed_backward(
        route_ids.T, route_gates.T, grad_out.T, hidden_acts[0, 0], down_weight[0].T
    )
    block = hidden_acts.shape[3] // lax.axis_size("dp")
    shift = weight_grad.shape[1] - block
    odd = lax.rem(lax.axis_index("dp"), 2) == 1
    weight_grad = jnp.where(odd, weight_grad[:, shift:], weight_grad[:, :block])
    return weight_grad.T[None], hidden_grad.T[None, None]


def solution(mesh):
    return jax.shard_map(
        on_device,
        mesh=mesh,
        in_specs=(
            P(("dp", "expert"), "tensor"),
            P(("dp", "expert"), None),
            P(("dp", "expert"), None),
            P("dp", "expert", None, None),
            P("expert", None, "tensor"),
        ),
        out_specs=(P("expert", "dp", "tensor"), P("dp", "expert", None, "tensor")),
        check_vma=False,
    )
```

```python
import jax
import jax.numpy as jnp
from jax import lax
from jax.experimental import pallas as pl
from jax.experimental.pallas import tpu as pltpu
from jax.sharding import PartitionSpec as P

BF, F32 = jnp.bfloat16, jnp.float32
MESH = pl.DeviceIdType.MESH
HOPS = (0, 1, -1, 2, -2, 3, -3, 4, -4, 5, -5, 6, -6, 7, -7, 8)
TURNS = (4, 3, -3, 2, -2, 1, -1, 0)
GROUPS = ((0, 256), (256, 128))
CAP = 24


def dot(a, b, dims=((1,), (0,))):
    return lax.dot_general(a, b, (dims, ((), ())), preferred_element_type=F32)


def kernel(
    ids_in, gates_in, grad_in, acts, weight_t, gw, gh,
    ids, gates, grad_t, staged, weight, acts_buf, fwd, outgoing, arrived, rows32, named, perm, total, done,
    *rest,
):
    ng = len(GROUPS)
    rt, peers, own, give, take, pa, pb, ma, mb = (rest[ng * i : ng * i + ng] for i in range(9))
    send_sems, recv_sems, local_sems = rest[9 * ng :]
    nx, nz, nt = lax.axis_size("dp"), lax.axis_size("expert"), lax.axis_size("tensor")
    ny = nt // 2
    x, z, t = lax.axis_index("dp"), lax.axis_index("expert"), lax.axis_index("tensor")
    core = lax.rem(t, 2)
    y = lax.div(t, 2)
    right, left = {"dp": lax.rem(x + 1, nx)}, {"dp": lax.rem(x + nx - 1, nx)}
    up, down = {"tensor": lax.rem(t + 2, nt)}, {"tensor": lax.rem(t + nt - 2, nt)}
    twin = {"tensor": t + 1 - 2 * core}
    chunk = weight.shape[0] // nt
    part_a = (chunk // 2 + 15) // 16 * 16
    rows_a, rows_b = pl.ds(0, part_a), pl.ds(part_a, chunk - part_a)
    count = [0]
    started = []

    def remote(src, dst, device):
        n = count[0]
        count[0] += 1
        return pltpu.make_async_remote_copy(
            src_ref=src, dst_ref=dst, send_sem=send_sems.at[n], recv_sem=recv_sems.at[n],
            device_id=device, device_id_type=MESH,
        )

    def start(copy):
        copy.start()
        started.append(copy)

    small = [pltpu.make_async_copy(src, dst, local_sems.at[3 + i]) for i, (src, dst) in enumerate(((ids_in, ids), (gates_in, gates), (grad_in, grad_t)))]
    for load in small:
        load.start()
    width = acts_buf.shape[3]
    load_weight = pltpu.make_async_copy(weight_t, staged, local_sems.at[0])
    load_weight.start()

    def column(owner, half):
        return pl.multiple_of((19 * owner // 2) * 128 + half * width, 128)

    loads = []
    for half in range(2):
        load = pltpu.make_async_copy(acts.at[:, pl.ds(column(x, half), width)], acts_buf.at[0, half], local_sems.at[1 + half])
        load.start()
        loads.append(load)

    barrier = pltpu.get_barrier_semaphore()
    experts = [lax.rem(z + nz - h, nz) for h in HOPS]
    greeted = [right, left, up, down, twin] + [{"expert": e} for e in experts[1:]]
    for device in greeted:
        pl.semaphore_signal(barrier, inc=1, device_id=device, device_id_type=MESH)

    for load in small:
        load.wait()
    id0, id1 = ids[0:1, :], ids[1:2, :]
    gate0, gate1 = gates[0:1, :], gates[1:2, :]
    tokens = ids.shape[1]
    for j, e in enumerate(experts):
        named[j : j + 1, :] = ((id0 == e) | (id1 == e)).astype(F32)
    earlier = lax.broadcasted_iota(jnp.int32, (tokens, tokens), 0) < lax.broadcasted_iota(jnp.int32, (tokens, tokens), 1)
    slots = dot(named[...].astype(BF), earlier.astype(F32).astype(BF)).astype(jnp.int32)
    place = lax.broadcasted_iota(jnp.int32, (CAP, tokens), 0)
    picks, scales = [], []
    for j, e in enumerate(experts):
        here = (slots[j : j + 1, :] == place) & (named[j : j + 1, :] > 0.5)
        gate = jnp.where(id0 == e, gate0, 0.0) + jnp.where(id1 == e, gate1, 0.0)
        picks.append(jnp.where(here, 1.0, 0.0))
        scales.append(jnp.sum(jnp.where(here, gate, 0.0), axis=1, keepdims=True))
    pick = jnp.concatenate(picks, axis=0).astype(BF)
    features = grad_t.shape[0]
    padded = rows32.shape[1]
    padded_grad = jnp.concatenate([grad_t[...], jnp.zeros((padded - features, tokens), BF)], axis=0)
    rows32[...] = dot(pick, padded_grad, ((1,), (1,))) * jnp.concatenate(scales, axis=0)
    lanes = padded // 128
    for j in range(nz):
        block = jnp.concatenate([rows32[CAP * j : CAP * (j + 1), 128 * i : 128 * (i + 1)] for i in range(lanes)], axis=0)
        if j == 0:
            arrived[0] = block.astype(BF)
        else:
            outgoing[j] = block.astype(BF)

    pl.semaphore_wait(barrier, len(greeted))

    to_expert = [None] + [remote(outgoing.at[j], arrived.at[j], {"expert": experts[j]}) for j in range(1, nz)]
    for copy in to_expert[1:]:
        start(copy)

    rows_here = acts.shape[0] // 2
    quarter = rows_here // 2
    first = pl.multiple_of(lax.rem(y, 2) * rows_here, 16)
    other = pl.multiple_of((1 - lax.rem(y, 2)) * rows_here, 16)
    far = lax.rem(x + 2, nx)
    x_near = []
    for q, device, owner in ((1, right, lax.rem(x + 1, nx)), (2, left, lax.rem(x + nx - 1, nx))):
        x_near.append(remote(
            acts.at[pl.ds(first, rows_here), pl.ds(column(owner, core), width)],
            acts_buf.at[q, core, pl.ds(first, rows_here), :], device,
        ))
    x_half, x_far = [], []
    for k, device in ((0, right), (1, left)):
        here = pl.ds(pl.multiple_of(first + k * quarter, 16), quarter)
        x_half.append(remote(acts.at[here, pl.ds(column(far, core), width)], fwd.at[k], device))
        x_far.append(remote(fwd.at[k], acts_buf.at[3, core, here, :], device))
    for copy in x_near + x_half:
        start(copy)
    y_part, twin_part = {}, {}
    for q in (1, 2, 3):
        for k, device in ((0, up), (1, down)):
            here = acts_buf.at[q, core, pl.ds(pl.multiple_of(first + k * quarter, 16), quarter), :]
            there = acts_buf.at[q, core, pl.ds(pl.multiple_of(other + k * quarter, 16), quarter), :]
            y_part[q, k] = remote(here, here, device)
            twin_part[q, k] = remote(there, there, twin)
        here = acts_buf.at[q, core, pl.ds(first, rows_here), :]
        twin_part[q, 2] = remote(here, here, twin)

    load_weight.wait()

    for at in range(0, weight.shape[0], 256):
        weight[at : at + 256, :] = staged[:, at : at + 256].T

    slot_count = perm.shape[1]
    stands = lax.broadcasted_iota(jnp.int32, (CAP, slot_count), 1) - lax.broadcasted_iota(jnp.int32, (CAP, slot_count), 0)
    perm[...] = jnp.concatenate(
        [jnp.where(stands == CAP * lax.rem(z + nz + h, nz), 1.0, 0.0) for h in HOPS], axis=0
    ).astype(BF)

    def near_acts():
        for q in (1, 2):
            x_near[q - 1].wait_recv()
            start(y_part[q, 0])
            start(y_part[q, 1])
            start(twin_part[q, 2])

    def half_acts():
        for k in range(2):
            x_half[k].wait_recv()
            start(x_far[k])

    def far_acts():
        for k in range(2):
            x_far[k].wait_recv()
            start(y_part[3, k])
        start(twin_part[3, 2])

    def shared_acts(q):
        for k in range(2):
            y_part[q, k].wait_recv()
            start(twin_part[q, k])

    to_peers = []
    for g, (low, size) in enumerate(GROUPS):
        top, bottom = pl.ds(0, features // 2), pl.ds(features // 2, features // 2)
        to_peers.append((
            remote(rt[g], peers[g].at[0], right),
            remote(rt[g], peers[g].at[1], left),
            remote(peers[g].at[0, top, :], peers[g].at[2, top, :], right),
            remote(peers[g].at[1, bottom, :], peers[g].at[2, bottom, :], left),
        ))
    unpacked = [0]

    def collect(g):
        low, size = GROUPS[g]
        until = -(-(low + size) // CAP)
        for j in range(unpacked[0], until):
            if j:
                to_expert[j].wait_recv()
            block = arrived[j].astype(F32)
            for i in range(lanes):
                rows32[CAP * j : CAP * (j + 1), 128 * i : 128 * (i + 1)] = block[CAP * i : CAP * (i + 1), :]
        unpacked[0] = until
        rt[g][...] = rows32[low : low + size, :].T[:features, :].astype(BF)
        start(to_peers[g][0])
        start(to_peers[g][1])

    def pass_on(g):
        for k in range(2):
            to_peers[g][k].wait_recv()
            start(to_peers[g][2 + k])

    index = {turn_: i for i, turn_ in enumerate(TURNS)}
    index[-4] = index[4]
    to_twin, rings = [], []
    for g in range(len(GROUPS)):
        to_twin.append([remote(give[g].at[i], take[g].at[i], twin) for i in range(ny)])
        ring = {}
        for s in range(4):
            ring["pa", s] = remote(own[g].at[index[4 - s], rows_a, :], pa[g].at[s], up)
            ring["mb", s] = remote(own[g].at[index[s - 4], rows_b, :], mb[g].at[s], down)
        for s in range(3):
            ring["pb", s] = remote(own[g].at[index[3 - s], rows_b, :], pb[g].at[s], up)
            ring["ma", s] = remote(own[g].at[index[s - 3], rows_a, :], ma[g].at[s], down)
        rings.append(ring)

    def product(g, i, side):
        at = pl.multiple_of(chunk * (2 * lax.rem(y + ny + TURNS[i], ny) + side), 16)
        return dot(weight[pl.ds(at, chunk), :], rt[g][...]).astype(BF)

    def prepare(g, *which):
        for i in which:
            give[g][i] = product(g, i, 1 - core)
            start(to_twin[g][i])
            own[g][i] = product(g, i, core)

    def join(g, *which):
        for i in which:
            to_twin[g][i].wait_recv()
            own[g][i] = (own[g][i].astype(F32) + take[g][i].astype(F32)).astype(BF)

    def step(g, name, s):
        ring = rings[g]
        ring[name, s].wait_recv()
        buffer = {"pa": pa, "pb": pb, "ma": ma, "mb": mb}[name][g]
        rows = rows_a if name[1] == "a" else rows_b
        reach = {"pa": 3 - s, "pb": 2 - s, "ma": s - 2, "mb": s - 3}[name]
        i = index[reach]
        own[g][i, rows, :] = (own[g][i, rows, :].astype(F32) + buffer[s].astype(F32)).astype(BF)
        start(ring[name, s + 1])

    def launch(g):
        ring = rings[g]
        join(g, 0)
        start(ring["pa", 0])
        start(ring["mb", 0])
        join(g, 1, 2)
        start(ring["pb", 0])
        start(ring["ma", 0])

    def advance(g, s):
        for name in ("pa", "mb") if s == 2 else ("pa", "mb", "pb", "ma"):
            step(g, name, s)

    def finish(g):
        low, size = GROUPS[g]
        ring = rings[g]
        for name, s in (("pb", 2), ("ma", 2), ("pa", 3), ("mb", 3)):
            ring[name, s].wait_recv()
        i = index[0]
        share_a = own[g][i, rows_a, :].astype(F32) + (pa[g][3].astype(F32) + ma[g][2].astype(F32))
        share_b = own[g][i, rows_b, :].astype(F32) + (pb[g][2].astype(F32) + mb[g][3].astype(F32))
        done[:, low : low + size] = jnp.concatenate([share_a, share_b], axis=0).astype(BF)

    def weight_grad(q):
        both = [r[...] for r in rt] if q == 0 else [r[q - 1] for r in peers]
        ordered = dot(jnp.concatenate(both, axis=1), perm[...]).astype(BF)
        for half in range(2):
            columns = pl.ds(half * width, width)
            added = dot(ordered, acts_buf[q, half])
            if q == 0:
                total[:, columns] = added
            elif q < 3:
                total[:, columns] += added
            else:
                gw[:, columns] = (total[:, columns] + added).astype(BF)

    near_acts()
    collect(0)
    prepare(0, 0, 1, 2, 3, 4)
    half_acts()
    launch(0)
    prepare(0, 5, 6, 7)
    join(0, 3, 4)
    shared_acts(1)
    shared_acts(2)
    advance(0, 0)
    join(0, 5, 6, 7)
    pass_on(0)
    far_acts()
    collect(1)
    prepare(1, 0, 1, 2)
    advance(0, 1)
    prepare(1, 3, 4)
    launch(1)
    prepare(1, 5, 6, 7)
    advance(0, 2)
    join(1, 3, 4)
    for load in loads:
        load.wait()
    weight_grad(0)
    pass_on(1)
    shared_acts(3)
    advance(1, 0)
    join(1, 5, 6, 7)
    finish(0)
    for k in range(3):
        twin_part[1, k].wait_recv()
    weight_grad(1)
    advance(1, 1)
    for k in range(3):
        twin_part[2, k].wait_recv()
    weight_grad(2)
    advance(1, 2)
    for k in range(3):
        twin_part[3, k].wait_recv()
    for g in range(ng):
        for k in range(2):
            to_peers[g][2 + k].wait_recv()
    weight_grad(3)
    finish(1)
    gh[...] = dot(done[...], perm[...]).astype(BF)
    for copy in started:
        copy.wait_send()


def routed_backward(ids, gates, grad_t, acts, weight_t):
    features, hidden = weight_t.shape
    slots = acts.shape[0]
    nx, nz, nt = lax.axis_size("dp"), lax.axis_size("expert"), lax.axis_size("tensor")
    width, chunk = 640, hidden // nt
    part_a = (chunk // 2 + 15) // 16 * 16
    part_b = chunk - part_a
    padded = -(-features // 128) * 128
    block = CAP * padded // 128
    sizes = [size for _, size in GROUPS]
    vmem = pltpu.VMEM
    scratch = [
        vmem(ids.shape, ids.dtype),
        vmem(gates.shape, gates.dtype),
        vmem(grad_t.shape, grad_t.dtype),
        vmem((features, hidden), BF),
        vmem((hidden, features), BF),
        vmem((nx, 2, slots, width), BF),
        vmem((2, slots // 4, width), BF),
        vmem((nz, block, 128), BF),
        vmem((nz, block, 128), BF),
        vmem((slots, padded), F32),
        vmem((nz, ids.shape[1]), F32),
        vmem((slots, slots), BF),
        vmem((features, 2 * width), F32),
        vmem((chunk, slots), BF),
    ]
    scratch += [vmem((features, n), BF) for n in sizes]
    scratch += [vmem((3, features, n), BF) for n in sizes]
    for _ in range(3):
        scratch += [vmem((nt // 2, chunk, n), BF) for n in sizes]
    for hops, rows in ((4, part_a), (3, part_b), (3, part_a), (4, part_b)):
        scratch += [vmem((hops, rows, n), BF) for n in sizes]
    copies = (nz - 1) + 6 + 15 + len(GROUPS) * (4 + nt // 2 + 14)
    scratch += [
        pltpu.SemaphoreType.DMA((copies,)),
        pltpu.SemaphoreType.DMA((copies,)),
        pltpu.SemaphoreType.DMA((6,)),
    ]
    away = pl.BlockSpec(memory_space=pltpu.HBM)
    return pl.pallas_call(
        kernel,
        out_shape=(
            jax.ShapeDtypeStruct((features, 2 * width), BF),
            jax.ShapeDtypeStruct((chunk, slots), BF),
        ),
        in_specs=[away] * 5,
        out_specs=(pl.BlockSpec(memory_space=pltpu.VMEM),) * 2,
        scratch_shapes=scratch,
        compiler_params=pltpu.CompilerParams(
            collective_id=0, has_side_effects=True, vmem_limit_bytes=52 * 1024 * 1024
        ),
        cost_estimate=pl.CostEstimate(flops=7 * 10**9, bytes_accessed=2 * 10**7, transcendentals=0),
    )(ids, gates, grad_t, acts, weight_t)


def on_device(grad_out, route_ids, route_gates, hidden_acts, down_weight):
    weight_grad, hidden_grad = routed_backward(
        route_ids.T, route_gates.T, grad_out.T, hidden_acts[0, 0], down_weight[0].T
    )
    block = hidden_acts.shape[3] // lax.axis_size("dp")
    shift = weight_grad.shape[1] - block
    odd = lax.rem(lax.axis_index("dp"), 2) == 1
    weight_grad = jnp.where(odd, weight_grad[:, shift:], weight_grad[:, :block])
    return weight_grad.T[None], hidden_grad.T[None, None]


def solution(mesh):
    return jax.shard_map(
        on_device,
        mesh=mesh,
        in_specs=(
            P(("dp", "expert"), "tensor"),
            P(("dp", "expert"), None),
            P(("dp", "expert"), None),
            P("dp", "expert", None, None),
            P("expert", None, "tensor"),
        ),
        out_specs=(P("expert", "dp", "tensor"), P("dp", "expert", None, "tensor")),
        check_vma=False,
    )
```
